32 devices in a mesh: sys: 2 (over y), row: 4 (over z), col: 4 (over x, core).
Axes of the slice: x: 2, y: 2, z: 4, core: 2. Of those that a mesh axis runs over, the one named last changes fastest.
Arguments:
- x_blocks: bfloat16 [80, 32, 128, 128], P(('sys', 'row'), 'col'), parts along dimension 0, may hold values from -6 to 6
- x_cols: int32 [80, 32], P(('sys', 'row'), 'col'), parts along dimension 0, may hold values from 0 to 39, as said below
- x_count: int32 [80, 4], P(('sys', 'row'), 'col'), parts along dimension 0, may hold values from 0 to 8, as said below
Outputs:
- updated: float32 [80, 32, 128, 128], P(('sys', 'row'), 'col'), parts along dimension 0
The draws below stay inside these ranges and needn't reach their ends.
There are 2 independent parts, one for each index of `sys`. The reference program is written for one: setup_inputs(seed, part) draws one part's arguments, and reference() takes and returns one part's arrays. A program takes and returns all parts, laid end to end along the dimension named above; each array names one. Nothing has to cross between parts.
Inputs may be any that keep to these rules, and one draw needn't show every extreme that they name: x_count[p, c] is the number of stored blocks of storage row p whose block column is congruent to c modulo 4. `x_cols`: for t below the count, slot c * 8 + t of storage row p names a distinct block column congruent to c modulo 4, in increasing order with t; other slots name arbitrary columns. Every stored block lies within 15 blocks of the diagonal, every diagonal block is stored, and the pattern is symmetric.
All inputs are finite; a program needn't handle non-finite values.
Results may differ from the reference program's by a relative error of at most 0.00057.
Values may be sent and summed in bfloat16 or wider, within the bound.
No kernel may reach another device: no remote copies, remote signals or barrier semaphores. Data moves between devices by JAX's collectives and lax.ppermute only.
A program may use at most 256 MiB of HBM per device.

```python
import jax
import jax.numpy as jnp
from jax import lax

B = 128
BR = 10
WMAX = 15
NB = 40
RT = 8
N_ROW = 4
N_COL = 4


def pattern(key):
    block_rows = BR * N_ROW
    reaches = jax.random.randint(jax.random.fold_in(key, 101), (block_rows,), 3, WMAX + 1)
    forced = jax.random.randint(jax.random.fold_in(key, 102), (), WMAX, block_rows - WMAX)
    reaches = jnp.where(jnp.arange(block_rows) == forced, WMAX, reaches).astype(jnp.int32)
    storage = jnp.arange(block_rows, dtype=jnp.int32)
    row_ids = storage % BR * N_ROW + storage // BR
    per_class = block_rows // N_COL
    residue = jnp.arange(N_COL, dtype=jnp.int32)
    column = residue[:, None] + N_COL * jnp.arange(per_class, dtype=jnp.int32)[None, :]
    row_grid = row_ids[:, None, None]
    limits = jnp.maximum(reaches[row_ids][:, None, None], reaches[column][None, :, :])
    present = jnp.abs(row_grid - column[None, :, :]) <= limits
    ranks = jnp.cumsum(present.astype(jnp.int32), axis=2)
    counts = ranks[:, :, -1].astype(jnp.int32)
    slot_rank = jnp.arange(RT, dtype=jnp.int32)
    chosen_hit = present[:, :, None, :] & (ranks[:, :, None, :] == slot_rank[None, None, :, None] + 1)
    picked = jnp.sum(jnp.where(chosen_hit, column[None, :, None, :], 0), axis=3)
    has_column = jnp.any(chosen_hit, axis=3)
    filler = residue[None, :, None] + N_COL * jax.random.randint(jax.random.fold_in(key, 103), (block_rows, N_COL, RT), 0, per_class)
    columns = jnp.where(has_column, picked, filler).astype(jnp.int32)
    return (columns.reshape(block_rows, N_COL * RT), counts)


def draw_x_cols(key, part):
    columns, counts = pattern(key)
    return columns


def draw_x_count(key, part):
    columns, counts = pattern(key)
    return counts


def block_levels(key, extent, pieces, least, largest):
    level = 1.0
    for position, parts in pieces:
        draws = jax.random.uniform(jax.random.fold_in(jax.random.fold_in(key, 6), position), (parts,), jnp.float32, least / len(pieces), largest / len(pieces))
        level = level * jnp.repeat(jnp.exp(draws), extent[position] // parts).reshape((-1,) + (1,) * (len(extent) - 1 - position))
    return level


def normal_values(stream_key, shape, scale, bound, split=(), kind=jnp.bfloat16):
    values = scale * jax.random.normal(stream_key, shape, jnp.float32)
    if split:
        values = values * block_levels(stream_key, shape, split, -0.22, 0.18)
    return jnp.clip(values, -bound, bound).astype(kind)


def setup_inputs(seed: int = 0, part: int = 0) -> dict:
    splits = jax.random.split(jax.random.key(seed), 4)
    own_keys = jax.random.split(jax.random.fold_in(splits[3], part), 4)
    return {
        "x_blocks": normal_values(own_keys[0], (NB, N_COL * RT, B, B), 1.0, 6.0, ((0, 4), (1, 4))),
        "x_cols": draw_x_cols(jax.random.fold_in(jax.random.fold_in(splits[3], part), 71), part),
        "x_count": draw_x_count(jax.random.fold_in(jax.random.fold_in(splits[3], part), 71), part),
    }


def product(left_blocks, left_cols, right_blocks, right_cols):
    block_rows, slot_total = right_cols.shape
    block_side = right_blocks.shape[-1]
    flattened = jnp.concatenate([right_blocks.reshape(-1, block_side, block_side), jnp.zeros((1, block_side, block_side), right_blocks.dtype)], axis=0)

    def one_row(operands):
        blocks, inner_cols, outer_cols = operands
        usable = inner_cols >= 0
        clipped = jnp.maximum(inner_cols, 0)
        where_row = ((clipped % N_ROW) * BR + clipped // N_ROW).astype(jnp.int32)
        candid = right_cols[where_row]
        matches = (candid[:, None, :] == outer_cols[None, :, None]) & usable[:, None, None] & (outer_cols[None, :, None] >= 0)
        choose = jnp.sum(jnp.where(matches, jnp.arange(slot_total, dtype=jnp.int32), 0), axis=2).astype(jnp.int32)
        located = jnp.any(matches, axis=2)
        picked = jnp.where(located, where_row[:, None] * slot_total + choose, block_rows * slot_total).astype(jnp.int32)
        chosen = flattened[picked].astype(jnp.float32)
        return jnp.einsum("sab,subc->uac", blocks.astype(jnp.float32), chosen)

    return lax.map(one_row, (left_blocks, left_cols, left_cols))


def reference(x_blocks, x_cols, x_count):
    slot_total = x_cols.shape[1]
    slot_ids = jnp.arange(slot_total, dtype=jnp.int32)
    stored = (slot_ids % RT)[None, :] < x_count[:, slot_ids // RT]
    own_cols = jnp.where(stored, x_cols, -1).astype(jnp.int32)
    first_sum = product(x_blocks, own_cols, x_blocks, own_cols)
    square = first_sum.astype(jnp.bfloat16)
    second = product(x_blocks, own_cols, square, own_cols)
    factor = 1.0 / (x_blocks.shape[-1] * (2 * WMAX + 1))
    updated = 1.5 * x_blocks.astype(jnp.float32) - 0.5 * factor * second
    return jnp.where(stored[:, :, None, None], updated, 0.0).astype(jnp.float32)
```

```python
import functools

import jax
import jax.numpy as jnp
import numpy as np
from jax import lax
from jax.experimental import pallas as pl
from jax.experimental.pallas import tpu as pltpu
from jax.sharding import PartitionSpec as P

WMAX = 15
FIELDS = 8
VMEM_BYTES = 60 * 2**20


def with_zero(panel_blocks):
    block_side = panel_blocks.shape[-1]
    flattened = panel_blocks.reshape(-1, block_side, block_side)
    return jnp.concatenate(
        [flattened, jnp.zeros((1, block_side, block_side), flattened.dtype)], axis=0
    )


def select_blocks(inner_cols, outer_cols, panel_cols, flattened, rows_per, row_devices):
    usable = inner_cols >= 0
    clipped = jnp.maximum(inner_cols, 0)
    where_row = clipped % row_devices * rows_per + clipped // row_devices
    candid = panel_cols[where_row]
    slot_count = panel_cols.shape[1]
    matches = (
        (candid[:, :, None, :] == outer_cols[:, None, :, None])
        & usable[:, :, None, None]
        & (outer_cols[:, None, :, None] >= 0)
    )
    choose = jnp.sum(jnp.where(matches, jnp.arange(slot_count, dtype=jnp.int32), 0), axis=3)
    located = jnp.any(matches, axis=3)
    picked = jnp.where(
        located, where_row[:, :, None] * slot_count + choose, panel_cols.shape[0] * slot_count
    )
    return flattened[picked]


def accumulate(row_blocks, inner_cols, outer_cols, panel_cols, flattened, rows_per, row_devices):
    chosen = select_blocks(inner_cols, outer_cols, panel_cols, flattened, rows_per, row_devices)
    return jnp.einsum("isab,isubc->iuac", row_blocks, chosen, preferred_element_type=jnp.float32)


def general_body(x_blocks, x_cols, x_count):
    rows_per, slot_count = x_cols.shape
    block_side = x_blocks.shape[-1]
    row_devices = lax.axis_size("row")
    stored = jnp.arange(slot_count, dtype=jnp.int32)[None, :] < x_count
    own_cols = jnp.where(stored, x_cols, -1)
    panel_blocks = lax.all_gather(x_blocks, "row", axis=0, tiled=True)
    panel_cols = lax.all_gather(own_cols, "row", axis=0, tiled=True)
    row_blocks = lax.all_gather(x_blocks, "col", axis=1, tiled=True)
    row_cols = lax.all_gather(own_cols, "col", axis=1, tiled=True)
    product = functools.partial(accumulate, row_blocks, row_cols, own_cols, panel_cols)
    square = product(with_zero(panel_blocks), rows_per, row_devices).astype(jnp.bfloat16)
    square_panel = lax.all_gather(square, "row", axis=0, tiled=True)
    second = product(with_zero(square_panel), rows_per, row_devices)
    factor = 1.0 / (block_side * (2 * WMAX + 1))
    updated = 1.5 * x_blocks.astype(jnp.float32) - 0.5 * factor * second
    return jnp.where(stored[:, :, None, None], updated, 0.0)


def pack_kernel(rows_per, count_ref, x_ref, packed_ref, sem):
    def one_row(p, offset):
        def one_slot(t, carry):
            pltpu.make_async_copy(x_ref.at[p, t], packed_ref.at[offset + t], sem).start()
            return carry

        lax.fori_loop(0, count_ref[p], one_slot, 0)
        return offset + count_ref[p]

    total = lax.fori_loop(0, rows_per, one_row, 0)

    def finish(m, carry):
        pltpu.make_async_copy(x_ref.at[0, 0], packed_ref.at[0], sem).wait()
        return carry

    lax.fori_loop(0, total, finish, 0)


def pack(x_blocks, x_count, capacity):
    rows_per, _, side, _ = x_blocks.shape
    return pl.pallas_call(
        functools.partial(pack_kernel, rows_per),
        out_shape=jax.ShapeDtypeStruct((capacity, side, side), x_blocks.dtype),
        grid_spec=pltpu.PrefetchScalarGridSpec(
            num_scalar_prefetch=1,
            grid=(1,),
            in_specs=[pl.BlockSpec(memory_space=pl.ANY)],
            out_specs=pl.BlockSpec(memory_space=pl.ANY),
            scratch_shapes=[pltpu.SemaphoreType.DMA],
        ),
    )(x_count.reshape(-1), x_blocks)


class Panels:
    def __init__(self, places, side, place_ref, sources):
        self.places, self.side = places, side
        self.place_ref, self.sources = place_ref, sources

    def window(self, ref, i, t):
        side = self.side
        return ref.at[
            pl.ds(pl.multiple_of(i * side, side), side),
            pl.ds(pl.multiple_of(t * side, side), side),
        ]

    def start(self, source, base, panel, sem):
        places, side = self.places, self.side
        blank = jnp.zeros((side, side), panel.dtype)

        def load_from(src):
            def one_row(i, started):
                for t in range(places):
                    slot = self.place_ref[base + i * places + t]

                    @pl.when(slot >= 0)
                    def _():
                        pltpu.make_async_copy(
                            src.at[slot], self.window(panel, i, t), sem
                        ).start()

                    @pl.when(slot < 0)
                    def _():
                        self.window(panel, i, t)[...] = blank

                    started = started + jnp.where(slot >= 0, 1, 0)
                return started

            return lambda: lax.fori_loop(0, places, one_row, 0)

        return lax.switch(source, [load_from(src) for src in self.sources])

    def finish(self, panel, count, sem):
        def one(m, carry):
            window = self.window(panel, 0, 0)
            pltpu.make_async_copy(self.sources[0].at[0], window, sem).wait()
            return carry

        lax.fori_loop(0, count, one, 0)


def band_pairs(places, reach):
    for j in range(0, places, 2):
        low, high = max(0, j - reach), min(places, j + 2 + reach)
        low, high = low // 2 * 2, min(places, -(-high // 2) * 2)
        for t in range(low, high, 2):
            yield j, t, max(low, t - reach), min(high, t + 2 + reach)


def multiply(total, left, right, places, reach, side):
    for j, t, low, high in band_pairs(places, reach):
        rows = pl.ds(low * side, (high - low) * side)
        inner = pl.ds(t * side, 2 * side)
        columns = pl.ds(j * side, 2 * side)
        total[rows, columns] += jnp.dot(
            left[rows, inner], right[inner, columns], preferred_element_type=jnp.float32
        )


def chain_kernel(
    places, reach, n_loads, n_sources, factor, task_ref, place_ref, slot_ref, *refs
):
    sources, (x_ref, out_ref) = refs[:n_sources], refs[n_sources : n_sources + 2]
    lefts, rights, totals, x_own, out_own, left_sem, right_sem, x_sem, out_sem = refs[
        n_sources + 2 :
    ]
    rows_per, slots, side, _ = x_own.shape
    panels = Panels(places, side, place_ref, sources)
    tasks_at = 1 + 2 * n_loads
    n_tasks = task_ref[0]

    def field(n, which):
        return task_ref[tasks_at + n * FIELDS + which]

    def start_left(n):
        here = lax.rem(n, 2)
        return panels.start(field(n, 0), field(n, 1), lefts.at[here], left_sem.at[here])

    x_copy = pltpu.make_async_copy(x_ref, x_own, x_sem)
    x_copy.start()
    first = start_left(0)
    counts = [
        panels.start(task_ref[1 + 2 * n], task_ref[2 + 2 * n], rights.at[n], right_sem)
        for n in range(n_loads)
    ]
    panels.finish(rights.at[0], sum(counts), right_sem)

    def one_task(n, count):
        here = lax.rem(n, 2)
        later = lax.cond(n + 1 < n_tasks, lambda: start_left(n + 1), lambda: 0)
        total = totals.at[field(n, 3)]

        @pl.when(field(n, 4) == 1)
        def _():
            total[...] = jnp.zeros_like(total)

        panels.finish(lefts.at[here], count, left_sem.at[here])
        multiply(total, lefts.at[here], rights.at[field(n, 2)], places, reach, side)

        @pl.when(field(n, 5) >= 0)
        def _():
            square = rights.at[field(n, 5)]

            def one_row(i, carry):
                for t in range(places):
                    slot = place_ref[field(n, 6) + i * places + t]
                    into, block = panels.window(square, i, t), panels.window(total, i, t)

                    @pl.when(slot >= 0)
                    def _():
                        into[...] = block[...].astype(square.dtype)

                    @pl.when(slot < 0)
                    def _():
                        into[...] = jnp.zeros((side, side), square.dtype)

                return carry

            lax.fori_loop(0, places, one_row, 0)

        return later

    lax.fori_loop(0, n_tasks, one_task, first)
    x_copy.wait()

    def one_row(i, carry):
        for s in range(slots):
            t = slot_ref[i * slots + s]

            @pl.when(t >= 0)
            def _():
                second = panels.window(totals.at[0], i, t)[...]
                out_own[i, s] = 1.5 * x_own[i, s].astype(jnp.float32) - factor * second

            @pl.when(t < 0)
            def _():
                out_own[i, s] = jnp.zeros((side, side), jnp.float32)

        pltpu.make_async_copy(out_own.at[i], out_ref.at[i], out_sem).start()
        return carry

    lax.fori_loop(0, rows_per, one_row, 0)
    pltpu.make_async_copy(out_own, out_ref, out_sem).wait()


def place_table(panel_cols, row_devices, capacity):
    devices, rows_per, wide = panel_cols.shape
    classes = row_devices
    slots = wide // classes
    cols = panel_cols.reshape(devices, rows_per, classes, slots).transpose(0, 2, 1, 3)
    counts = jnp.sum(cols >= 0, axis=3, dtype=jnp.int32)
    offsets = jnp.cumsum(counts, axis=2) - counts
    at = jnp.arange(rows_per, dtype=jnp.int32)[:, None]
    match = (cols[:, :, :, None, :] // classes == at) & (cols[:, :, :, None, :] >= 0)
    rank = jnp.sum(jnp.where(match, jnp.arange(slots, dtype=jnp.int32) + 1, 0), axis=4)
    return jnp.where(rank > 0, offsets[:, :, :, None] + rank - 1, -1)


def shard_capacity(devices, rows_per, slots):
    at = np.arange(rows_per)
    gap = devices * (at[:, None] - at[None, :])
    most = max(
        int((abs(gap + shift) <= WMAX).sum()) for shift in range(1 - devices, devices)
    )
    return min(most, rows_per * slots)


def task_tables(devices, area):
    tables = []
    for r in range(devices):
        for c in range(devices):
            loads = [[0, (l * devices + c) * area] for l in range(devices)]
            tasks = []
            for k in range(devices):
                for l in range(devices):
                    last = l == devices - 1
                    tasks.append(
                        [
                            0,
                            (k * devices + l) * area,
                            l,
                            0,
                            int(l == 0),
                            devices + k if last else -1,
                            (k * devices + c) * area,
                            0,
                        ]
                    )
            for k in range(devices):
                tasks.append([0, (r * devices + k) * area, devices + k, 0, int(k == 0), -1, 0, 0])
            tables.append(np.concatenate([[len(tasks)], np.ravel(loads), np.ravel(tasks)]))
    return np.stack(tables).astype(np.int32)


def square_body(x_blocks, x_cols, x_count):
    rows_per, slots = x_cols.shape
    side = x_blocks.shape[-1]
    devices = lax.axis_size("row")
    places = rows_per
    reach = (WMAX + devices - 1) // devices
    capacity = shard_capacity(devices, rows_per, slots)
    packed = pack(x_blocks, x_count, capacity)
    stored = jnp.arange(slots, dtype=jnp.int32)[None, :] < x_count
    own_cols = jnp.where(stored, x_cols, -1)
    slot_table = jnp.where(stored, x_cols // devices, -1).reshape(-1)
    panel_cols = lax.all_gather(own_cols, ("row", "col"), axis=0)
    gathered = lax.all_gather(packed, ("row", "col"), axis=0, tiled=True)
    panel_cols = panel_cols.reshape(devices, devices, rows_per, slots)
    panel_cols = panel_cols.transpose(0, 2, 1, 3).reshape(devices, rows_per, devices * slots)
    places_at = place_table(panel_cols, devices, capacity)
    shard = jnp.arange(devices * devices, dtype=jnp.int32).reshape(devices, devices, 1, 1)
    places_at = jnp.where(places_at >= 0, places_at + shard * capacity, -1).reshape(-1)
    mine = lax.axis_index("row") * devices + lax.axis_index("col")
    tasks = jnp.asarray(task_tables(devices, rows_per * rows_per))[mine]
    factor = 0.5 / (side * (2 * WMAX + 1))
    order = rows_per * side
    return pl.pallas_call(
        functools.partial(chain_kernel, places, reach, devices, 1, factor),
        out_shape=jax.ShapeDtypeStruct(x_blocks.shape, jnp.float32),
        grid_spec=pltpu.PrefetchScalarGridSpec(
            num_scalar_prefetch=3,
            grid=(1,),
            in_specs=[pl.BlockSpec(memory_space=pl.ANY)] * 2,
            out_specs=pl.BlockSpec(memory_space=pl.ANY),
            scratch_shapes=[
                pltpu.VMEM((2, order, order), jnp.bfloat16),
                pltpu.VMEM((2 * devices, order, order), jnp.bfloat16),
                pltpu.VMEM((1, order, order), jnp.float32),
                pltpu.VMEM(x_blocks.shape, x_blocks.dtype),
                pltpu.VMEM(x_blocks.shape, jnp.float32),
                pltpu.SemaphoreType.DMA((2,)),
                pltpu.SemaphoreType.DMA,
                pltpu.SemaphoreType.DMA,
                pltpu.SemaphoreType.DMA,
            ],
        ),
        compiler_params=pltpu.CompilerParams(vmem_limit_bytes=VMEM_BYTES),
    )(tasks, places_at, slot_table, gathered, x_blocks)


def solution(mesh):
    def body(x_blocks, x_cols, x_count):
        rows_per = x_cols.shape[0]
        if mesh.shape["row"] == mesh.shape["col"] and rows_per % 2 == 0:
            return square_body(x_blocks, x_cols, x_count)
        return general_body(x_blocks, x_cols, x_count)

    placed = (
        P(("sys", "row"), "col", None, None),
        P(("sys", "row"), "col"),
        P(("sys", "row"), "col"),
    )
    return jax.shard_map(
        body,
        mesh=mesh,
        in_specs=placed,
        out_specs=P(("sys", "row"), "col", None, None),
        check_vma=False,
    )
```

```python
import functools
import typing

import jax
import jax.numpy as jnp
import numpy as np
from jax import lax
from jax.experimental import pallas as pl
from jax.experimental.pallas import tpu as pltpu
from jax.sharding import PartitionSpec as P

WMAX = 15
FIELDS = 8
TAIL = 16
VMEM_BYTES = 60 * 2**20


def with_zero(panel_blocks):
    block_side = panel_blocks.shape[-1]
    flattened = panel_blocks.reshape(-1, block_side, block_side)
    return jnp.concatenate(
        [flattened, jnp.zeros((1, block_side, block_side), flattened.dtype)], axis=0
    )


def select_blocks(inner_cols, outer_cols, panel_cols, flattened, rows_per, row_devices):
    usable = inner_cols >= 0
    clipped = jnp.maximum(inner_cols, 0)
    where_row = clipped % row_devices * rows_per + clipped // row_devices
    candid = panel_cols[where_row]
    slot_count = panel_cols.shape[1]
    matches = (
        (candid[:, :, None, :] == outer_cols[:, None, :, None])
        & usable[:, :, None, None]
        & (outer_cols[:, None, :, None] >= 0)
    )
    choose = jnp.sum(jnp.where(matches, jnp.arange(slot_count, dtype=jnp.int32), 0), axis=3)
    located = jnp.any(matches, axis=3)
    picked = jnp.where(
        located, where_row[:, :, None] * slot_count + choose, panel_cols.shape[0] * slot_count
    )
    return flattened[picked]


def accumulate(row_blocks, inner_cols, outer_cols, panel_cols, flattened, rows_per, row_devices):
    chosen = select_blocks(inner_cols, outer_cols, panel_cols, flattened, rows_per, row_devices)
    return jnp.einsum("isab,isubc->iuac", row_blocks, chosen, preferred_element_type=jnp.float32)


def general_body(x_blocks, x_cols, x_count):
    rows_per, slot_count = x_cols.shape
    block_side = x_blocks.shape[-1]
    row_devices = lax.axis_size("row")
    stored = jnp.arange(slot_count, dtype=jnp.int32)[None, :] < x_count
    own_cols = jnp.where(stored, x_cols, -1)
    panel_blocks = lax.all_gather(x_blocks, "row", axis=0, tiled=True)
    panel_cols = lax.all_gather(own_cols, "row", axis=0, tiled=True)
    row_blocks = lax.all_gather(x_blocks, "col", axis=1, tiled=True)
    row_cols = lax.all_gather(own_cols, "col", axis=1, tiled=True)
    product = functools.partial(accumulate, row_blocks, row_cols, own_cols, panel_cols)
    square = product(with_zero(panel_blocks), rows_per, row_devices).astype(jnp.bfloat16)
    square_panel = lax.all_gather(square, "row", axis=0, tiled=True)
    second = product(with_zero(square_panel), rows_per, row_devices)
    factor = 1.0 / (block_side * (2 * WMAX + 1))
    updated = 1.5 * x_blocks.astype(jnp.float32) - 0.5 * factor * second
    return jnp.where(stored[:, :, None, None], updated, 0.0)


def band_rows(places, reach, upper):
    before, after = (reach - 1, reach) if upper else (reach, reach - 1)
    return [(max(0, i - before), min(places, i + after + 1)) for i in range(places)]


def band_offsets(places, reach, upper):
    widths = [high - low for low, high in band_rows(places, reach, upper)]
    return [sum(widths[:i]) for i in range(places + 1)]


def pack_kernel(reach, cols_ref, count_ref, x_ref, packed_ref, held, sem):
    rows_per, slots, side, _ = x_ref.shape
    devices = lax.axis_size("row")
    upper = lax.axis_index("row") >= lax.axis_index("col")
    lane = lax.broadcasted_iota(jnp.int32, (TAIL, side), 1)
    tail = jnp.zeros((TAIL, side), jnp.float32)
    held[...] = jnp.zeros_like(held)
    rows = [band_rows(rows_per, reach, kind) for kind in (True, False)]
    offsets = [band_offsets(rows_per, reach, kind) for kind in (True, False)]
    total = 0
    for i in range(rows_per):
        begin = jnp.where(upper, *(at[i] - low[i][0] for at, low in zip(offsets, rows)))
        count = count_ref[i, 0]
        for s in range(slots):
            column = cols_ref[i, s] // devices
            tail = jnp.where((lane == i * rows_per + column) & (s < count), 1.0, tail)

            @pl.when(s < count)
            def _():
                into = held.at[pl.ds(pl.multiple_of((begin + column) * side, side), side)]
                pltpu.make_async_copy(x_ref.at[i, s], into, sem).start()

        total = total + count
    held[pl.ds(held.shape[0] - TAIL, TAIL)] = tail.astype(held.dtype)

    def finish(m, carry):
        pltpu.make_async_copy(x_ref.at[0, 0], held.at[pl.ds(0, side)], sem).wait()
        return carry

    lax.fori_loop(0, total, finish, 0)
    copy = pltpu.make_async_copy(held, packed_ref, sem)
    copy.start()
    copy.wait()


def pack(x_blocks, x_cols, x_count, reach):
    rows_per, _, side, _ = x_blocks.shape
    shape = (band_offsets(rows_per, reach, True)[-1] * side + TAIL, side)
    return pl.pallas_call(
        functools.partial(pack_kernel, reach),
        out_shape=jax.ShapeDtypeStruct(shape, x_blocks.dtype),
        grid_spec=pltpu.PrefetchScalarGridSpec(
            num_scalar_prefetch=2,
            grid=(1,),
            in_specs=[pl.BlockSpec(memory_space=pl.ANY)],
            out_specs=pl.BlockSpec(memory_space=pl.ANY),
            scratch_shapes=[pltpu.VMEM(shape, x_blocks.dtype), pltpu.SemaphoreType.DMA],
        ),
    )(x_cols, x_count, x_blocks)


def outer_places(places, reach):
    return [(i, t) for i in range(places) for t in range(places) if abs(i - t) == reach + 1]


class Panels:
    def __init__(self, side, places, reach, sources):
        self.side, self.places, self.reach, self.sources = side, places, reach, sources
        self.tall = sources[0].shape[0] - TAIL

    def rows(self, i, count=1):
        start = i * self.side
        start = start if isinstance(i, int) else pl.multiple_of(start, self.side)
        return pl.ds(start, count * self.side)

    def start(self, source, upper, panel, sem):
        blank = jnp.zeros((self.side, self.side), panel.dtype)
        for i, t in outer_places(self.places, self.reach):
            panel[t, self.rows(i)] = blank
        for kind in (True, False):
            rows = band_rows(self.places, self.reach, kind)
            offsets = band_offsets(self.places, self.reach, kind)

            @pl.when(upper == int(kind))
            def _():
                for i in range(self.places):
                    t = i - self.reach if kind else i + self.reach
                    if 0 <= t < self.places:
                        panel[t, self.rows(i)] = blank

            for at, src in enumerate(self.sources):

                @pl.when((source == at) & (upper == int(kind)))
                def _():
                    band = src.at[pl.ds(0, self.tall)].reshape(-1, self.side, self.side)
                    for i, (low, high) in enumerate(rows):
                        blocks = band.at[pl.ds(offsets[i], high - low)]
                        into = panel.at[pl.ds(low, high - low), self.rows(i)]
                        pltpu.make_async_copy(blocks, into, sem).start()

    def finish(self, sem):
        band = self.sources[0].at[pl.ds(0, self.tall)]
        pltpu.make_async_copy(band, band, sem).wait()

    def part(self, panel, first, last, low, high):
        rows = self.rows(low, high - low)
        return jnp.concatenate([panel[t, rows] for t in range(first, last)], axis=1)


def pairs_near(first, last, places, reach):
    low, high = max(0, first - reach), min(places, last + reach)
    return low // 2 * 2, min(places, -(-high // 2) * 2)


def multiply(panels, total, left, right):
    places, reach = panels.places, panels.reach
    for j in range(0, places, 2):
        low, high = pairs_near(j, j + 2, places, reach)
        for i in range(low, high, 2):
            start, stop = pairs_near(i, i + 2, places, reach)
            start, stop = max(start, low), min(stop, high)
            total[panels.rows(i, 2), panels.rows(j, 2)] += jnp.dot(
                panels.part(left, start, stop, i, i + 2),
                panels.part(right, j, j + 2, start, stop),
                preferred_element_type=jnp.float32,
            )


def chain_kernel(plan, reach, factor, task_ref, cols_ref, count_ref, *refs):
    sources, rest = refs[: plan.sources], list(refs[plan.sources :])
    totals_in = rest.pop(0) if plan.totals_in else None
    x_ref = rest.pop(0) if plan.last else None
    out_ref = rest.pop(0)
    rights, lefts, totals, mask, right_sem, left_sem, mask_sem, in_sem, out_sem = rest[:9]
    x_own, out_own = rest[9:] if plan.last else (None, None)
    side = sources[0].shape[-1]
    places = totals.shape[1] // side
    panels = Panels(side, places, reach, sources)
    tasks_at = 1 + 2 * plan.loads
    devices = lax.axis_size("row")
    mine = lax.axis_index("row") * devices + lax.axis_index("col")
    n_tasks = task_ref[mine, 0]

    def field(n, which):
        return task_ref[mine, tasks_at + n * FIELDS + which]

    def start_left(n):
        here = lax.rem(n, 2)
        panels.start(field(n, 0), field(n, 1), lefts.at[here], left_sem.at[here])

    def strips(source, target, sem, act):
        for i in range(0, places, 2):
            low, high = pairs_near(i, i + 2, places, reach)
            band = (panels.rows(i, 2), panels.rows(low, high - low))
            act(pltpu.make_async_copy(source.at[band], target.at[band], sem))

    def incoming(at, act):
        which, where = plan.totals_in[at]
        strips(totals_in.at[which], totals.at[where], in_sem.at[at], act)

    def outgoing(at, act):
        strips(totals.at[plan.totals_out[at]], out_ref.at[at], out_sem.at[at], act)

    def start_right(n):
        panels.start(
            task_ref[mine, 1 + 2 * n], task_ref[mine, 2 + 2 * n], rights.at[n], right_sem.at[n]
        )

    start_left(0)
    start_right(0)
    if plan.last:
        incoming(0, lambda copy: copy.start())
        x_copy = pltpu.make_async_copy(x_ref, x_own, out_sem.at[1])

    def round_square(n):
        square = rights.at[field(n, 5)]
        summed = totals.at[1 if plan.last else field(n, 5)]
        for at, src in enumerate(sources):

            @pl.when(field(n, 6) == at)
            def _():
                under = src.at[pl.ds(panels.tall, TAIL)]
                pltpu.make_async_copy(under, mask, mask_sem).start()

        pltpu.make_async_copy(sources[0].at[pl.ds(panels.tall, TAIL)], mask, mask_sem).wait()
        held = mask[...].astype(jnp.float32)[:1]
        for i in range(places):
            for t in range(max(0, i - reach - 1), min(places, i + reach + 2)):
                flag = held[:, i * places + t : i * places + t + 1]
                block = summed[panels.rows(i), panels.rows(t)]
                block = jnp.where(jnp.broadcast_to(flag, block.shape) > 0, block, 0.0)
                square[t, panels.rows(i)] = block.astype(square.dtype)

    def one_task(n, carry):
        here = lax.rem(n, 2)
        flags = field(n, 7)

        panels.finish(left_sem.at[here])

        @pl.when(flags // 64 == 1)
        def _():
            panels.finish(right_sem.at[field(n, 2)])

        @pl.when(n + 1 < n_tasks)
        def _():
            start_left(n + 1)

        @pl.when(n + 1 < plan.loads)
        def _():
            start_right(n + 1)

        for at in range(int(plan.last), len(plan.totals_in)):

            @pl.when(n == at - int(plan.last))
            def _():
                incoming(at, lambda copy: copy.start())
                if plan.last:
                    x_copy.start()

        for at in range(len(plan.totals_in)):

            @pl.when(flags % 8 == at)
            def _():
                incoming(at, lambda copy: copy.wait())

        if plan.rounds:

            @pl.when(field(n, 5) >= 0)
            def _():
                round_square(n)

        total = totals.at[field(n, 3)]

        @pl.when(field(n, 4) == 1)
        def _():
            for i in range(0, places, 2):
                low, high = pairs_near(i, i + 2, places, reach)
                band = (panels.rows(i, 2), panels.rows(low, high - low))
                total[band] = jnp.zeros(total.at[band].shape, total.dtype)

        multiply(panels, total, lefts.at[here], rights.at[field(n, 2)])
        for at in range(len(plan.totals_out)):

            @pl.when(flags // 8 % 8 == at)
            def _():
                outgoing(at, lambda copy: copy.start())

        return carry

    lax.fori_loop(0, n_tasks, one_task, 0)
    if not plan.last:
        for at in range(len(plan.totals_out)):
            outgoing(at, lambda copy: copy.wait())
        return

    x_copy.wait()
    rows_per, slots = x_own.shape[:2]

    def one_row(i, carry):
        for s in range(slots):
            t = cols_ref[i, s] // devices

            @pl.when(s < count_ref[i, 0])
            def _():
                second = totals[0, panels.rows(i), panels.rows(t)]
                out_own[i, s] = 1.5 * x_own[i, s].astype(jnp.float32) - factor * second

            @pl.when(s >= count_ref[i, 0])
            def _():
                out_own[i, s] = jnp.zeros((side, side), jnp.float32)

        pltpu.make_async_copy(out_own.at[i], out_ref.at[i], out_sem.at[0]).start()
        return carry

    lax.fori_loop(0, rows_per, one_row, 0)
    pltpu.make_async_copy(out_own, out_ref, out_sem.at[0]).wait()


class Plan(typing.NamedTuple):
    sources: int
    loads: int
    totals: int
    totals_in: tuple
    totals_out: tuple
    rounds: bool
    last: bool


def chain(plan, reach, factor, table, pattern, sources, totals_in, x_blocks):
    side = sources[0].shape[1]
    places = x_blocks.shape[0]
    order = places * side
    operands = list(sources) + ([totals_in] if plan.totals_in else [])
    scratch = [
        pltpu.VMEM((max(4, plan.loads), places, order, side), jnp.bfloat16),
        pltpu.VMEM((2, places, order, side), jnp.bfloat16),
        pltpu.VMEM((plan.totals, order, order), jnp.float32),
        pltpu.VMEM((TAIL, side), jnp.bfloat16),
        pltpu.SemaphoreType.DMA((4,)),
        pltpu.SemaphoreType.DMA((2,)),
        pltpu.SemaphoreType.DMA,
        pltpu.SemaphoreType.DMA((4,)),
        pltpu.SemaphoreType.DMA((4,)),
    ]
    if plan.last:
        operands.append(x_blocks)
        scratch.append(pltpu.VMEM(x_blocks.shape, x_blocks.dtype))
        scratch.append(pltpu.VMEM(x_blocks.shape, jnp.float32))
        shape = x_blocks.shape
    else:
        shape = (len(plan.totals_out), order, order)
    return pl.pallas_call(
        functools.partial(chain_kernel, plan, reach, factor),
        out_shape=jax.ShapeDtypeStruct(shape, jnp.float32),
        grid_spec=pltpu.PrefetchScalarGridSpec(
            num_scalar_prefetch=3,
            grid=(1,),
            in_specs=[pl.BlockSpec(memory_space=pl.ANY)] * len(operands),
            out_specs=pl.BlockSpec(memory_space=pl.ANY),
            scratch_shapes=scratch,
        ),
        compiler_params=pltpu.CompilerParams(vmem_limit_bytes=VMEM_BYTES),
        cost_estimate=pl.CostEstimate(
            flops=10**8, bytes_accessed=10**5, transcendentals=0
        ),
    )(table, *pattern, *operands)


def arrivals(row):
    near, far = row ^ 1, 3 - row
    return (row, near, far, far ^ 1) if row in MID else (row, near, far ^ 1, far)


def sources_of(row, col):
    rows = arrivals(row)
    if row in MID:
        names = ("a sa xa sxa", "b sb g1 sg1", "m1 sm1 g2 sg2", "m2 sm2 g3 sg3")
    else:
        last = "p1 sp2" if col % 2 == 0 else "p2 sp1"
        names = ("a sa xa sxa", "b sb g2 sg2", "g1 sg1 g3 sg3", "f2 sf2 " + last)
    return {
        (rows[kq], col ^ lq): name
        for kq in range(4)
        for lq, name in enumerate(names[kq].split())
    }


def stage_tables():
    stages = [[], [], []]
    for r in range(4):
        for c in range(4):
            where, rows = sources_of(r, c), arrivals(r)
            near = [l for l in rows if l >> 1 == c >> 1]
            far = [l for l in rows if l not in near]
            known = list(rows[:3])
            early = [l for l in known if l in near]
            late = [l for l in rows if l not in early]

            def terms(kq, inner, total=None, zero=True, wait=7, out=7):
                k, total = rows[kq], kq if total is None else total
                tasks = [[where[k, l], int(k >= l), l, total, 0, -1, "", 63] for l in inner]
                tasks[0][4] = int(zero)
                tasks[0][7] += wait - 7
                tasks[-1][7] += 8 * (out - 7)
                return tasks

            def final(kq, zero=False, wait=7, out=7):
                k = rows[kq]
                flags = wait + 8 * out
                return [[where[r, k], int(r >= k), kq, 0, int(zero), kq, where[k, c], flags]]

            def add(at, tasks):
                loads = []
                for task in tasks:
                    if task[5] < 0:
                        if task[2] not in loads:
                            loads.append(task[2])
                            task[7] += 64
                        task[2] = loads.index(task[2])
                panels = [(where[l, c], int(l >= c)) for l in loads]
                stages[at].append((panels, tasks))

            tasks = terms(0, known, out=0) + terms(1, known, out=1)
            add(0, tasks + terms(2, early, out=2))
            tasks = terms(3, near, out=1)
            tasks += terms(0, [rows[3]], zero=False, wait=0)
            tasks += terms(1, [rows[3]], zero=False, wait=1)
            tasks += terms(2, late, zero=False, wait=2)
            add(1, tasks + final(0, zero=True) + final(1) + final(2, out=0))
            tasks = terms(3, far, total=1, zero=False, wait=0)
            add(2, tasks + final(3, wait=1))

    names, tables = [], []
    for stage in stages:
        used = {name for loads, _ in stage for name, _ in loads}
        used |= {task[0] for _, tasks in stage for task in tasks}
        used |= {task[6] for _, tasks in stage for task in tasks}
        used = sorted(used - {""})
        rows = []
        for loads, tasks in stage:
            row = [len(tasks)]
            for name, upper in loads:
                row += [used.index(name), upper]
            for task in tasks:
                mask = used.index(task[6]) if task[6] else 0
                row += [used.index(task[0]), *task[1:6], mask, task[7]]
            rows.append(row)
        width = max(map(len, rows))
        tables.append(np.array([row + [0] * (width - len(row)) for row in rows], np.int32))
        names.append(used)
    return names, tables


def make_plans(names):
    return (
        Plan(len(names[0]), 3, 3, (), (0, 1, 2), False, False),
        Plan(len(names[1]), 4, 4, ((0, 0), (1, 1), (2, 2)), (0, 3), True, False),
        Plan(len(names[2]), 2, 2, ((1, 1), (0, 0)), (), True, True),
    )


def permute(array, moves):
    pairs = [(a * 4 + b, c * 4 + d) for (a, b), (c, d) in moves]
    return lax.ppermute(array, ("row", "col"), pairs)


def across(array, rows, shift, cols=range(4)):
    return permute(array, [((r, c), (r, c ^ shift)) for r in rows for c in cols])


def along(array, hops, cols=range(4)):
    return permute(array, [((a, c), (b, c)) for a, b in hops for c in cols])


PAIRS = ((0, 1), (1, 0), (2, 3), (3, 2))
MIDDLE = ((1, 2), (2, 1))
OUTWARD = ((1, 0), (2, 3))
ALL, MID, END = (0, 1, 2, 3), (1, 2), (0, 3)


def square_body(x_blocks, x_cols, x_count):
    side = x_blocks.shape[-1]
    devices = lax.axis_size("row")
    reach = (WMAX + devices - 1) // devices
    factor = 0.5 / (side * (2 * WMAX + 1))
    h = {"a": pack(x_blocks, x_cols, x_count, reach)}
    row = lax.axis_index("row")
    middle = (row == 1) | (row == 2)
    names, tables = stage_tables()
    plans = make_plans(names)
    pattern = (x_cols, x_count)

    def stage(at, totals_in=None):
        sources = [h[name] for name in names[at]]
        table = jnp.asarray(tables[at])
        return chain(plans[at], reach, factor, table, pattern, sources, totals_in, x_blocks)

    def settle(*extra):
        keys = sorted(h)
        values = lax.optimization_barrier([*(h[key] for key in keys), *extra])
        h.update(zip(keys, values))
        return values[len(keys) :]

    h["b"] = along(h["a"], PAIRS)
    h["m1"] = along(h["a"], MIDDLE)
    h["xa"] = across(h["a"], ALL, 2)
    h["sa"] = across(h["a"], ALL, 1)
    inward = jnp.where(middle, h["m1"], h["xa"])
    beside = jnp.where(middle, h["m1"], h["b"])
    inward, beside = settle(inward, beside)

    h["g1"] = along(inward, PAIRS)
    h["g2"] = across(beside, ALL, 2)
    h["m2"] = along(h["b"], MIDDLE)
    h["sxa"] = across(h["xa"], ALL, 1)
    h["sb"] = across(h["b"], ALL, 1)
    h["sm1"] = across(h["m1"], MID, 1)
    (beside,) = settle(jnp.where(middle, h["m2"], h["g1"]))

    h["f2"] = along(h["m2"], OUTWARD)
    h["g3"] = across(beside, ALL, 2)
    h["sg1"] = across(h["g1"], ALL, 1)
    h["sg2"] = across(h["g2"], ALL, 1)
    h["sm2"] = across(h["m2"], MID, 1)
    (totals,) = settle(stage(0))

    p1 = across(h["f2"], END, 2, (0, 2))
    p2 = along(h["g3"], OUTWARD, (1, 3))
    h["sf2"] = across(h["f2"], END, 1)
    h["sg3"] = across(h["g3"], ALL, 1)
    totals, h["p1"], h["p2"] = settle(stage(1, totals), p1, p2)
    h["sp1"] = across(h["p1"], END, 1, (0, 2))
    h["sp2"] = across(h["p2"], END, 1, (1, 3))
    return stage(2, totals)


def solution(mesh):
    def body(x_blocks, x_cols, x_count):
        rows_per = x_cols.shape[0]
        if mesh.shape["row"] == mesh.shape["col"] == 4 and rows_per % 2 == 0:
            return square_body(x_blocks, x_cols, x_count)
        return general_body(x_blocks, x_cols, x_count)

    placed = (
        P(("sys", "row"), "col", None, None),
        P(("sys", "row"), "col"),
        P(("sys", "row"), "col"),
    )
    return jax.shard_map(
        body,
        mesh=mesh,
        in_specs=placed,
        out_specs=P(("sys", "row"), "col", None, None),
        check_vma=False,
    )
```
